512 devices in a mesh: band: 256 (over y, x_hi, z, core), grid: 2 (over x_lo).
Axes of the slice: x: 4 (x_hi: 2, x_lo: 2; x = x_hi * 2 + x_lo), y: 8, z: 8, core: 2. Of those that a mesh axis runs over, the one named last changes fastest.
Arguments:
- orbitals: float32 [256, 64, 4096], P('band', 'grid'), may hold values from -1.8 to 1.8
Outputs:
- exchange_partial: float32 [256, 64, 4096], P('band', 'grid')
The draws below stay inside these ranges and needn't reach their ends.
All inputs are finite; a program needn't handle non-finite values.
Results may differ from the reference program's by a relative error of at most 0.0044.
Values may be sent and summed in bfloat16 or wider, within the bound.
No kernel may reach another device: no remote copies, remote signals or barrier semaphores. Data moves between devices by JAX's collectives and lax.ppermute only.
A program may use at most 64 MiB of HBM per device.

```python
import math
import jax
import jax.numpy as jnp
import numpy as np
from jax import lax

NG = 64
BPD = 1
REACH = 2
BANDS = 256
N_BAND = 256


def draw_orbitals(key, part):
    key = jax.random.fold_in(key, 7)
    shape = (BANDS, NG, NG * NG)
    value = 0.4 * jax.random.truncated_normal(key, -4.5, 4.5, shape, jnp.float32)
    return value


def setup_inputs(seed: int = 0) -> dict:
    arg_keys = jax.random.split(jax.random.key(seed), 2)
    orbitals = draw_orbitals(jax.random.fold_in(arg_keys[1], 71), 0)
    return {"orbitals": orbitals}


coulomb = 46.9 * 46.9 / math.pi
highest = lax.Precision.HIGHEST


def settle(value):
    return lax.optimization_barrier(value.astype(jnp.bfloat16)).astype(jnp.float32)


def tables():
    count = jnp.arange(NG, dtype=jnp.int32)
    product = (count[:, None] * count[None, :]) % NG
    angle = (2.0 * math.pi / NG) * product.astype(jnp.float32)
    cas = jnp.cos(angle) + jnp.sin(angle)
    folded = jnp.where(count < NG // 2, count, count - NG)
    square = folded * folded
    msq = (square[:, None, None] + square[None, :, None] + square[None, None, :]).astype(jnp.float32)
    kernel = jnp.where(msq > 0.0, coulomb / jnp.maximum(msq, 1.0), 0.0).astype(jnp.float32)
    return cas, kernel


def poisson(rho, cas, kernel):
    pairs, rows = rho.shape[0], rho.shape[1]
    cas_low = settle(cas)
    field = rho.reshape(pairs, rows, NG, NG)
    spec = jnp.einsum('pxyz,zk->pxyk', field, cas, precision=highest)
    spec = settle(jnp.einsum('pxyk,yl->pxlk', spec, cas, precision=highest))
    screened = jnp.einsum('pxlk,xm->pmlk', spec, cas_low, precision=highest) * kernel
    screened = settle(jnp.einsum('pmlk,mx->pxlk', screened, cas, precision=highest))
    result = jnp.einsum('pxlk,ly->pxyk', screened, cas, precision=highest)
    result = jnp.einsum('pxyk,kz->pxyz', result, cas, precision=highest)
    return (result * (1.0 / NG**3)).reshape(pairs, rows, NG * NG)


def reference(orbitals):
    blocks = orbitals.reshape(N_BAND, BPD, NG, NG * NG)
    cas, kernel = tables()
    upper = np.triu_indices(BPD)
    index_map = np.zeros((BPD, BPD), dtype=np.int32)
    for position in range(len(upper[0])):
        index_map[upper[0][position], upper[1][position]] = position
        index_map[upper[1][position], upper[0][position]] = position
    flat_map = jnp.asarray(index_map.reshape(-1))

    def owner(place):
        own = lax.dynamic_index_in_dim(blocks, place, 0, keepdims=False)
        solved = poisson(own[upper[0]] * own[upper[1]], cas, kernel)
        full = solved[flat_map].reshape(BPD, BPD, NG, NG * NG)
        mine = -jnp.sum(full * own[None], axis=1)
        returned = []
        for step in range(1, REACH + 1):
            other = ((place + step) % N_BAND).astype(jnp.int32)
            visit = lax.dynamic_index_in_dim(blocks, other, 0, keepdims=False)
            rho = (own[:, None] * visit[None]).reshape(BPD * BPD, NG, NG * NG)
            cross = poisson(rho, cas, kernel).reshape(BPD, BPD, NG, NG * NG)
            mine = mine - jnp.sum(cross * visit[None], axis=1)
            returned.append(-jnp.sum(cross * own[:, None], axis=0))
        return mine, jnp.stack(returned)

    mine, back = lax.map(owner, jnp.arange(N_BAND, dtype=jnp.int32))
    total = mine
    for step in range(1, REACH + 1):
        total = total + jnp.roll(back[:, step - 1], step, axis=0)
    return total.reshape(BANDS, NG, NG * NG)
```

```python
import math

import jax
import jax.numpy as jnp
import numpy as np
from jax import lax
from jax.experimental import pallas as pl
from jax.experimental.pallas import tpu as pltpu
from jax.sharding import PartitionSpec as P

NG = 64
REACH = 2
NEAR = 0
ROWS = NG // 2
PLANE = NG * NG
LANES = 2 * NG
BLOCKS = PLANE // LANES
CODE = 64.0
CHUNK = 8
WIDTH = 1024
coulomb = 46.9 * 46.9 / math.pi


def cas_table():
    count = np.arange(NG)
    angle = 2.0 * math.pi / NG * (count[:, None] * count[None, :] % NG)
    return np.cos(angle) + np.sin(angle)


def split(table):
    high = table.astype(jnp.bfloat16)
    low = (table - high.astype(np.float64)).astype(jnp.bfloat16)
    return high, low


def plane_matrix():
    cas = cas_table()
    high, low = split(np.block([[cas, cas], [cas, -cas]]))
    return np.concatenate([high, low], axis=1)


def x_matrices():
    cas = cas_table()
    high, low = split(cas)
    return high, np.concatenate([high, high, low], axis=1)


def kernel_table():
    count = np.arange(NG)
    folded = np.where(count < NG // 2, count, count - NG)
    square = (folded * folded).astype(np.float64)
    block, upper, last = np.meshgrid(
        np.arange(BLOCKS), np.arange(2), np.arange(NG), indexing="ij"
    )
    column = (square[block + BLOCKS * upper] + square[last]).reshape(1, PLANE)
    msq = square[:, None] + column
    table = np.where(msq > 0.0, coulomb / np.maximum(msq, 1.0), 0.0) / NG**3
    return table.astype(np.float32)


def hartley(items):
    n = len(items)
    if n == 1:
        return items
    even, odd = hartley(items[0::2]), hartley(items[1::2])
    half = n // 2
    turned = list(odd)
    for k in range(1, (half + 1) // 2):
        c, s = math.cos(2.0 * math.pi * k / n), math.sin(2.0 * math.pi * k / n)
        a, b = odd[k], odd[half - k]
        if 8 * k == n:
            turned[k], turned[half - k] = (a + b) * c, (a - b) * c
        else:
            turned[k], turned[half - k] = a * c + b * s, a * s - b * c
    return [e + t for e, t in zip(even, turned)] + [e - t for e, t in zip(even, turned)]


def twist(items):
    n = len(items)
    low_lanes = lax.broadcasted_iota(jnp.int32, items[0].shape, 1) < NG
    out = [None] * n
    out[0] = items[0]
    for k in range(1, n // 2):
        c, s = math.cos(math.pi * k / n), math.sin(math.pi * k / n)
        a, b = items[k], items[n - k]
        out[k] = jnp.where(low_lanes, a, a * c + b * s)
        out[n - k] = jnp.where(low_lanes, b, a * s - b * c)
    out[n // 2] = items[n // 2]
    return out


def decoded(code):
    return jnp.log2(code.astype(jnp.float32)) * (1.0 / CODE)


def lane_block(b):
    return slice(b * LANES, (b + 1) * LANES)


def pairwise(items):
    while len(items) > 1:
        items = [a + b for a, b in zip(items[0::2], items[1::2])]
    return items[0]


def pairwise(items):
    while len(items) > 1:
        items = [a + b for a, b in zip(items[0::2], items[1::2])]
    return items[0]


def encode_kernel(psi_ref, code_ref, marked_ref):
    psi = psi_ref[0]
    code = jnp.exp2(psi * CODE).astype(jnp.bfloat16)
    code_ref[...] = code
    marked_ref[:, :PLANE] = code
    part = pairwise([psi[:, lane_block(b)] ** 2 for b in range(BLOCKS)])
    coarse = jnp.round(part * 512.0) * (1.0 / 512.0)
    total = jnp.sum(coarse, axis=1, keepdims=True) + jnp.sum(part - coarse, axis=1, keepdims=True)
    marked_ref[:, PLANE:] = jnp.broadcast_to(total, (ROWS, LANES)).astype(jnp.bfloat16)


def forward(mine, other, plane_ref, spec_ref, scratch):
    for tile in range(NG // 8):
        slab, row = divmod(8 * tile, ROWS)
        rows = slice(row, row + 8)
        fields = [
            mine[slab][rows, lane_block(b)] * other[slab][rows, lane_block(b)]
            for b in range(BLOCKS)
        ]
        for b, item in enumerate(twist(hartley(fields))):
            scratch[b * NG + 8 * tile : b * NG + 8 * tile + 8, :] = item
    for first in range(0, BLOCKS, CHUNK):
        value = scratch[first * NG : (first + CHUNK) * NG, :]
        high = value.astype(jnp.bfloat16)
        low = (value - high.astype(jnp.float32)).astype(jnp.bfloat16)
        operand = jnp.concatenate([high, low], axis=1)
        both = jnp.dot(operand, plane_ref[...], preferred_element_type=jnp.float32)
        spec = (both[:, :LANES] + both[:, LANES:]).astype(jnp.bfloat16)
        for b in range(CHUNK):
            spec_ref[:, lane_block(first + b)] = spec[b * NG : (b + 1) * NG]


def screen(spec_ref, low_ref, wide_ref, table_ref, rows):
    for first in range(0, PLANE, WIDTH):
        lanes = slice(first, first + WIDTH)
        value = jnp.dot(low_ref[...], spec_ref[:, lanes], preferred_element_type=jnp.float32)
        value = value * table_ref[:, lanes]
        high = value.astype(jnp.bfloat16)
        low = (value - high.astype(jnp.float32)).astype(jnp.bfloat16)
        operand = jnp.concatenate([high, low, high], axis=0)
        result = jnp.dot(wide_ref[:rows], operand, preferred_element_type=jnp.float32)
        spec_ref[:rows, lanes] = result.astype(jnp.bfloat16)


def inverse(spec_ref, plane_ref, scratch, rows, use):
    for first in range(0, BLOCKS, CHUNK):
        operand = jnp.concatenate(
            [spec_ref[:rows, lane_block(first + b)] for b in range(CHUNK)], axis=0
        )
        both = jnp.dot(operand, plane_ref[:LANES], preferred_element_type=jnp.float32)
        scratch[first * rows : (first + CHUNK) * rows, :] = both[:, :LANES] + both[:, LANES:]
    for tile in range(rows // 8):
        fields = [scratch[b * rows + 8 * tile : b * rows + 8 * tile + 8, :] for b in range(BLOCKS)]
        slab, row = divmod(8 * tile, ROWS)
        for b, item in enumerate(hartley(twist(fields))):
            use(slab, slice(row, row + 8), lane_block(b), item)


def copy_kernel(code_ref, out_ref):
    out_ref[...] = code_ref[...]


def self_kernel(psi_ref, mine_ref, beside_ref, plane_ref, low_ref, wide_ref, table_ref,
                beside_out, total_out, spec, scratch):
    beside_out[...] = decoded(beside_ref[:, :PLANE])
    band = (psi_ref.at[0], beside_out)
    forward(band, band, plane_ref, spec, scratch)
    first = lax.broadcasted_iota(jnp.int32, (ROWS, LANES), 1) == 0
    for rows, ref in ((slice(0, ROWS), mine_ref), (slice(ROWS, NG), beside_ref)):
        spec[rows, :LANES] = jnp.where(first, ref[:, PLANE:], spec[rows, :LANES])
    screen(spec, low_ref, wide_ref, table_ref, ROWS)

    def use(slab, rows, lanes, item):
        total_out[rows, lanes] = psi_ref[0, rows, lanes] * item

    inverse(spec, plane_ref, scratch, ROWS, use)


def pair_kernel(psi_ref, beside_ref, same_ref, cross_ref, plane_ref, low_ref, wide_ref,
                table_ref, part_ref, total_out, beside_out, same_out, cross_out,
                other, spec, scratch, sums):
    other[0] = decoded(same_ref[...])
    other[1] = decoded(cross_ref[...])
    band = (psi_ref.at[0], beside_ref)
    forward(band, (other.at[0], other.at[1]), plane_ref, spec, scratch)
    screen(spec, low_ref, wide_ref, table_ref, NG)

    def use(slab, rows, lanes, item):
        part = other[slab, rows, lanes] * item
        if slab == 0:
            total_out[rows, lanes] = part_ref[rows, lanes] + part
        else:
            sums[2, rows, lanes] = part
        sums[slab, rows, lanes] = band[slab][rows, lanes] * item

    inverse(spec, plane_ref, scratch, NG, use)
    same_out[...] = sums[0].astype(jnp.bfloat16)
    cross_out[...] = sums[1].astype(jnp.bfloat16)
    beside_out[...] = sums[2].astype(jnp.bfloat16)


vmem = pl.BlockSpec(memory_space=pltpu.VMEM)
limit = pltpu.CompilerParams(vmem_limit_bytes=40 * 1024 * 1024)


def shape(dims, dtype):
    return jax.ShapeDtypeStruct(dims, dtype)


def call(kernel, outs, *args, scratch=()):
    return pl.pallas_call(
        kernel, out_shape=outs, in_specs=[vmem] * len(args),
        out_specs=jax.tree.map(lambda _: vmem, outs),
        scratch_shapes=scratch, compiler_params=limit,
    )(*args)


def on_device(orbitals):
    bands = lax.axis_size("band")
    axes = ("band", "grid")

    def route(flip):
        pairs = []
        for band in range(bands):
            for g in range(2):
                other = (band - (1 if g == NEAR else REACH)) % bands
                pairs.append((2 * other + (1 - g if flip else g), 2 * band + g))
        return pairs

    def home(flip):
        return [(b, a) for a, b in route(flip)]

    swap = [(0, 1), (1, 0)]
    plane = jnp.asarray(plane_matrix())
    stacked = jnp.concatenate([plane, plane], axis=0)
    x_low, x_wide = (jnp.asarray(m) for m in x_matrices())
    table = jnp.asarray(kernel_table())
    tables = (stacked, x_low, x_wide, table)

    sent = shape((ROWS, PLANE), jnp.bfloat16)
    field = shape((ROWS, PLANE), jnp.float32)
    spec = pltpu.VMEM((NG, PLANE), jnp.bfloat16)
    work = pltpu.VMEM((BLOCKS * NG, LANES), jnp.float32)
    marks = shape((ROWS, PLANE + LANES), jnp.bfloat16)

    code, marked = call(encode_kernel, (sent, marks), orbitals)
    same = lax.ppermute(code, axes, route(False))
    cross = lax.ppermute(code, axes, route(True))
    marked = call(copy_kernel, marks, marked)
    beside = lax.ppermute(marked, "grid", swap)
    beside, total = call(
        self_kernel, (field, field), orbitals, marked, beside, *tables, scratch=[spec, work]
    )
    total, beside, same, cross = call(
        pair_kernel, (field, sent, sent, sent),
        orbitals, beside, same, cross, *tables, total,
        scratch=[
            pltpu.VMEM((2, ROWS, PLANE), jnp.float32), spec, work,
            pltpu.VMEM((3, ROWS, PLANE), jnp.float32),
        ],
    )
    for share in (
        lax.ppermute(beside, "grid", swap),
        lax.ppermute(same, axes, home(False)),
        lax.ppermute(cross, axes, home(True)),
    ):
        total = total + share.astype(jnp.float32)
    return -total[None]


def solution(mesh):
    in_specs = (P("band", "grid", None),)
    out_specs = P("band", "grid", None)
    return jax.shard_map(
        on_device, mesh=mesh, in_specs=in_specs, out_specs=out_specs, check_vma=False
    )
```

```python
import math

import jax
import jax.numpy as jnp
import numpy as np
from jax import lax
from jax.experimental import pallas as pl
from jax.experimental.pallas import tpu as pltpu
from jax.sharding import PartitionSpec as P

NG = 64
REACH = 2
NEAR = 0
ROWS = NG // 2
PLANE = NG * NG
LANES = 2 * NG
BLOCKS = PLANE // LANES
CODE = 64.0
CHUNK = 8
WIDTH = 1024
coulomb = 46.9 * 46.9 / math.pi


def cas_table():
    count = np.arange(NG)
    angle = 2.0 * math.pi / NG * (count[:, None] * count[None, :] % NG)
    return np.cos(angle) + np.sin(angle)


def split(table):
    high = table.astype(jnp.bfloat16)
    low = (table - high.astype(np.float64)).astype(jnp.bfloat16)
    return high, low


def plane_matrix():
    cas = cas_table()
    high, low = split(np.block([[cas, cas], [cas, -cas]]))
    return np.concatenate([high, low], axis=1)


def x_matrices():
    cas = cas_table()
    high, low = split(cas)
    return high, np.concatenate([high, high, low], axis=1)


def column_squares():
    count = np.arange(NG)
    folded = np.where(count < NG // 2, count, count - NG)
    square = (folded * folded).astype(np.float32)
    block, upper, last = np.meshgrid(
        np.arange(BLOCKS), np.arange(2), np.arange(NG), indexing="ij"
    )
    return (square[block + BLOCKS * upper] + square[last]).reshape(1, PLANE)


def hartley(items):
    n = len(items)
    if n == 1:
        return items
    even, odd = hartley(items[0::2]), hartley(items[1::2])
    half = n // 2
    turned = list(odd)
    for k in range(1, (half + 1) // 2):
        c, s = math.cos(2.0 * math.pi * k / n), math.sin(2.0 * math.pi * k / n)
        a, b = odd[k], odd[half - k]
        if 8 * k == n:
            turned[k], turned[half - k] = (a + b) * c, (a - b) * c
        else:
            turned[k], turned[half - k] = a * c + b * s, a * s - b * c
    return [e + t for e, t in zip(even, turned)] + [e - t for e, t in zip(even, turned)]


def twist(items):
    n = len(items)
    low_lanes = lax.broadcasted_iota(jnp.int32, items[0].shape, 1) < NG
    out = [None] * n
    out[0] = items[0]
    for k in range(1, n // 2):
        c, s = math.cos(math.pi * k / n), math.sin(math.pi * k / n)
        a, b = items[k], items[n - k]
        out[k] = jnp.where(low_lanes, a, a * c + b * s)
        out[n - k] = jnp.where(low_lanes, b, a * s - b * c)
    out[n // 2] = items[n // 2]
    return out


def decoded(code):
    return jnp.log2(code.astype(jnp.float32)) * (1.0 / CODE)


def lane_block(b):
    return slice(b * LANES, (b + 1) * LANES)


def pairwise(items):
    while len(items) > 1:
        items = [a + b for a, b in zip(items[0::2], items[1::2])]
    return items[0]


def pairwise(items):
    while len(items) > 1:
        items = [a + b for a, b in zip(items[0::2], items[1::2])]
    return items[0]


def encode_kernel(psi_ref, code_ref, marked_ref):
    psi = psi_ref[0]
    code = jnp.exp2(psi * CODE).astype(jnp.bfloat16)
    code_ref[...] = code
    marked_ref[:, :PLANE] = code
    part = pairwise([psi[:, lane_block(b)] ** 2 for b in range(BLOCKS)])
    coarse = jnp.round(part * 512.0) * (1.0 / 512.0)
    total = jnp.sum(coarse, axis=1, keepdims=True) + jnp.sum(part - coarse, axis=1, keepdims=True)
    marked_ref[:, PLANE:] = jnp.broadcast_to(total, (ROWS, LANES)).astype(jnp.bfloat16)


def forward(mine, other, plane_ref, spec_ref, scratch):
    for tile in range(NG // 8):
        slab, row = divmod(8 * tile, ROWS)
        rows = slice(row, row + 8)
        fields = [
            mine[slab][rows, lane_block(b)] * other[slab][rows, lane_block(b)]
            for b in range(BLOCKS)
        ]
        for b, item in enumerate(twist(hartley(fields))):
            scratch[b * NG + 8 * tile : b * NG + 8 * tile + 8, :] = item
    for first in range(0, BLOCKS, CHUNK):
        value = scratch[first * NG : (first + CHUNK) * NG, :]
        high = value.astype(jnp.bfloat16)
        low = (value - high.astype(jnp.float32)).astype(jnp.bfloat16)
        operand = jnp.concatenate([high, low], axis=1)
        both = jnp.dot(operand, plane_ref[...], preferred_element_type=jnp.float32)
        spec = (both[:, :LANES] + both[:, LANES:]).astype(jnp.bfloat16)
        for b in range(CHUNK):
            spec_ref[:, lane_block(first + b)] = spec[b * NG : (b + 1) * NG]


def screen(spec_ref, low_ref, wide_ref, column_ref, rows):
    count = lax.broadcasted_iota(jnp.int32, (NG, WIDTH), 0)
    folded = jnp.where(count < NG // 2, count, count - NG)
    square = (folded * folded).astype(jnp.float32)
    for first in range(0, PLANE, WIDTH):
        lanes = slice(first, first + WIDTH)
        msq = square + column_ref[:, lanes]
        scaled = (coulomb / NG**3) / jnp.maximum(msq, 1.0)
        value = jnp.dot(low_ref[...], spec_ref[:, lanes], preferred_element_type=jnp.float32)
        value = value * jnp.where(msq > 0.0, scaled, 0.0)
        high = value.astype(jnp.bfloat16)
        low = (value - high.astype(jnp.float32)).astype(jnp.bfloat16)
        operand = jnp.concatenate([high, low, high], axis=0)
        result = jnp.dot(wide_ref[:rows], operand, preferred_element_type=jnp.float32)
        spec_ref[:rows, lanes] = result.astype(jnp.bfloat16)


def inverse(spec_ref, plane_ref, scratch, rows, use):
    for first in range(0, BLOCKS, CHUNK):
        operand = jnp.concatenate(
            [spec_ref[:rows, lane_block(first + b)] for b in range(CHUNK)], axis=0
        )
        both = jnp.dot(operand, plane_ref[:LANES], preferred_element_type=jnp.float32)
        scratch[first * rows : (first + CHUNK) * rows, :] = both[:, :LANES] + both[:, LANES:]
    for tile in range(rows // 8):
        fields = [scratch[b * rows + 8 * tile : b * rows + 8 * tile + 8, :] for b in range(BLOCKS)]
        slab, row = divmod(8 * tile, ROWS)
        for b, item in enumerate(hartley(twist(fields))):
            use(slab, slice(row, row + 8), lane_block(b), item)


def copy_kernel(code_ref, out_ref):
    out_ref[...] = code_ref[...]


def pair_kernel(cross_ref, same_ref, beside_code, psi_ref, plane_ref, low_ref, wide_ref,
                column_ref, part_out, field_out, beside_out, same_out, cross_out,
                other, spec, scratch, sums):
    other[0] = decoded(same_ref[...])
    other[1] = decoded(cross_ref[...])
    field_out[...] = decoded(beside_code[:, :PLANE])
    band = (psi_ref.at[0], field_out)
    forward(band, (other.at[0], other.at[1]), plane_ref, spec, scratch)
    screen(spec, low_ref, wide_ref, column_ref, NG)

    def use(slab, rows, lanes, item):
        part = other[slab, rows, lanes] * item
        if slab == 0:
            part_out[rows, lanes] = part
        else:
            sums[2, rows, lanes] = part
        sums[slab, rows, lanes] = band[slab][rows, lanes] * item

    inverse(spec, plane_ref, scratch, NG, use)
    same_out[...] = sums[0].astype(jnp.bfloat16)
    cross_out[...] = sums[1].astype(jnp.bfloat16)
    beside_out[...] = sums[2].astype(jnp.bfloat16)


def self_kernel(psi_ref, mine_ref, beside_code, field_ref, plane_ref, low_ref, wide_ref,
                column_ref, part_ref, total_out, spec, scratch):
    band = (psi_ref.at[0], field_ref)
    forward(band, band, plane_ref, spec, scratch)
    first = lax.broadcasted_iota(jnp.int32, (ROWS, LANES), 1) == 0
    for rows, ref in ((slice(0, ROWS), mine_ref), (slice(ROWS, NG), beside_code)):
        spec[rows, :LANES] = jnp.where(first, ref[:, PLANE:], spec[rows, :LANES])
    screen(spec, low_ref, wide_ref, column_ref, ROWS)

    def use(slab, rows, lanes, item):
        total_out[rows, lanes] = part_ref[rows, lanes] + psi_ref[0, rows, lanes] * item

    inverse(spec, plane_ref, scratch, ROWS, use)


vmem = pl.BlockSpec(memory_space=pltpu.VMEM)
limit = pltpu.CompilerParams(vmem_limit_bytes=14 * 1024 * 1024)


def shape(dims, dtype):
    return jax.ShapeDtypeStruct(dims, dtype)


def call(kernel, outs, *args, scratch=()):
    return pl.pallas_call(
        kernel, out_shape=outs, in_specs=[vmem] * len(args),
        out_specs=jax.tree.map(lambda _: vmem, outs),
        scratch_shapes=scratch, compiler_params=limit,
    )(*args)


def on_device(orbitals):
    bands = lax.axis_size("band")
    axes = ("band", "grid")

    def route(flip):
        pairs = []
        for band in range(bands):
            for g in range(2):
                other = (band - (1 if g == NEAR else REACH)) % bands
                pairs.append((2 * other + (1 - g if flip else g), 2 * band + g))
        return pairs

    def home(flip):
        return [(b, a) for a, b in route(flip)]

    swap = [(0, 1), (1, 0)]
    plane = jnp.asarray(plane_matrix())
    stacked = jnp.concatenate([plane, plane], axis=0)
    x_low, x_wide = (jnp.asarray(m) for m in x_matrices())
    column = jnp.asarray(column_squares())
    tables = (stacked, x_low, x_wide, column)

    sent = shape((ROWS, PLANE), jnp.bfloat16)
    field = shape((ROWS, PLANE), jnp.float32)
    spec = pltpu.VMEM((NG, PLANE), jnp.bfloat16)
    work = pltpu.VMEM((BLOCKS * NG, LANES), jnp.float32)
    marks = shape((ROWS, PLANE + LANES), jnp.bfloat16)

    code, marked = call(encode_kernel, (sent, marks), orbitals)
    same = lax.ppermute(code, axes, route(False))
    cross = lax.ppermute(code, axes, route(True))
    marked = call(copy_kernel, marks, marked)
    beside = lax.ppermute(marked, "grid", swap)
    part, partner, beside_share, same, cross = call(
        pair_kernel, (field, field, sent, sent, sent),
        cross, same, beside, orbitals, *tables,
        scratch=[
            pltpu.VMEM((2, ROWS, PLANE), jnp.float32), spec, work,
            pltpu.VMEM((3, ROWS, PLANE), jnp.float32),
        ],
    )
    total = call(
        self_kernel, field, orbitals, marked, beside, partner, *tables, part,
        scratch=[spec, work],
    )
    for share in (
        lax.ppermute(cross, axes, home(True)),
        lax.ppermute(same, axes, home(False)),
        lax.ppermute(beside_share, "grid", swap),
    ):
        total = total + share.astype(jnp.float32)
    return -total[None]


def solution(mesh):
    in_specs = (P("band", "grid", None),)
    out_specs = P("band", "grid", None)
    return jax.shard_map(
        on_device, mesh=mesh, in_specs=in_specs, out_specs=out_specs, check_vma=False
    )
```

```python
import math

import jax
import jax.numpy as jnp
import numpy as np
from jax import lax
from jax.experimental import pallas as pl
from jax.experimental.pallas import tpu as pltpu
from jax.sharding import PartitionSpec as P

NG = 64
REACH = 2
NEAR = 0
ROWS = NG // 2
PLANE = NG * NG
LANES = 2 * NG
BLOCKS = PLANE // LANES
CODE = 64.0
CHUNK = 8
WIDTH = 1024
coulomb = 46.9 * 46.9 / math.pi


def cas_table():
    count = np.arange(NG)
    angle = 2.0 * math.pi / NG * (count[:, None] * count[None, :] % NG)
    return np.cos(angle) + np.sin(angle)


def split(table):
    high = table.astype(jnp.bfloat16)
    low = (table - high.astype(np.float64)).astype(jnp.bfloat16)
    return high, low


def plane_matrix():
    cas = cas_table()
    high, low = split(np.block([[cas, cas], [cas, -cas]]))
    return np.concatenate([high, low], axis=1)


def x_matrices():
    cas = cas_table()
    high, low = split(cas)
    return high, np.concatenate([high, high, low], axis=1)


def column_squares():
    count = np.arange(NG)
    folded = np.where(count < NG // 2, count, count - NG)
    square = (folded * folded).astype(np.float32)
    block, upper, last = np.meshgrid(
        np.arange(BLOCKS), np.arange(2), np.arange(NG), indexing="ij"
    )
    return (square[block + BLOCKS * upper] + square[last]).reshape(1, PLANE)


def hartley(items):
    n = len(items)
    if n == 1:
        return items
    even, odd = hartley(items[0::2]), hartley(items[1::2])
    half = n // 2
    turned = list(odd)
    for k in range(1, (half + 1) // 2):
        c, s = math.cos(2.0 * math.pi * k / n), math.sin(2.0 * math.pi * k / n)
        a, b = odd[k], odd[half - k]
        if 8 * k == n:
            turned[k], turned[half - k] = (a + b) * c, (a - b) * c
        else:
            turned[k], turned[half - k] = a * c + b * s, a * s - b * c
    return [e + t for e, t in zip(even, turned)] + [e - t for e, t in zip(even, turned)]


def twist(items):
    n = len(items)
    low_lanes = lax.broadcasted_iota(jnp.int32, items[0].shape, 1) < NG
    out = [None] * n
    out[0] = items[0]
    for k in range(1, n // 2):
        c, s = math.cos(math.pi * k / n), math.sin(math.pi * k / n)
        a, b = items[k], items[n - k]
        out[k] = jnp.where(low_lanes, a, a * c + b * s)
        out[n - k] = jnp.where(low_lanes, b, a * s - b * c)
    out[n // 2] = items[n // 2]
    return out


def decoded(code):
    return jnp.log2(code.astype(jnp.float32)) * (1.0 / CODE)


def lane_block(b):
    return slice(b * LANES, (b + 1) * LANES)


def encode_kernel(psi_ref, code_ref, wide_ref):
    code = jnp.exp2(psi_ref[0] * CODE).astype(jnp.bfloat16)
    code_ref[...] = code
    wide_ref[:, :PLANE] = code
    wide_ref[:, PLANE:] = jnp.zeros((ROWS, 2 * LANES), jnp.bfloat16)


def mark_kernel(psi_ref, code_ref, marked_ref, turned):
    group = LANES // ROWS
    for t in range(BLOCKS // group):
        squares = [psi_ref[0, :, lane_block(t * group + k)] ** 2 for k in range(group)]
        turned[t * LANES : (t + 1) * LANES, :] = jnp.concatenate(squares, axis=0).T
    chains = 2 * BLOCKS // group
    along_z = turned[pl.ds(0, chains, stride=NG), :]
    for z in range(1, NG):
        along_z = along_z + turned[pl.ds(z, chains, stride=NG), :]
    shifted = [along_z] + [
        pltpu.roll(along_z, LANES - k * ROWS, axis=1) for k in range(1, group)
    ]
    total = None
    for t in range(BLOCKS // group):
        for k in range(group):
            for e in range(2):
                row = shifted[k][2 * t + e : 2 * t + e + 1]
                total = row if total is None else total + row
    marked_ref[:, :PLANE] = code_ref[...]
    column = jnp.broadcast_to(total, (LANES, LANES)).T[:ROWS]
    marked_ref[:, PLANE:] = column.astype(jnp.bfloat16)


def forward(mine, other, plane_ref, spec_ref, first_row, scratch):
    for tile in range(ROWS // 8):
        rows = slice(8 * tile, 8 * tile + 8)
        fields = [mine[rows, lane_block(b)] * other[rows, lane_block(b)] for b in range(BLOCKS)]
        for b, item in enumerate(twist(hartley(fields))):
            scratch[b * ROWS + 8 * tile : b * ROWS + 8 * tile + 8, :] = item
    for first in range(0, BLOCKS, CHUNK):
        value = scratch[first * ROWS : (first + CHUNK) * ROWS, :]
        high = value.astype(jnp.bfloat16)
        low = (value - high.astype(jnp.float32)).astype(jnp.bfloat16)
        operand = jnp.concatenate([high, low], axis=1)
        both = jnp.dot(operand, plane_ref[...], preferred_element_type=jnp.float32)
        spec = (both[:, :LANES] + both[:, LANES:]).astype(jnp.bfloat16)
        for b in range(CHUNK):
            spec_ref[first_row : first_row + ROWS, lane_block(first + b)] = (
                spec[b * ROWS : (b + 1) * ROWS]
            )


def screen(spec_ref, low_ref, wide_ref, column_ref, rows):
    count = lax.broadcasted_iota(jnp.int32, (NG, WIDTH), 0)
    folded = jnp.where(count < NG // 2, count, count - NG)
    square = (folded * folded).astype(jnp.float32)
    for first in range(0, PLANE, WIDTH):
        lanes = slice(first, first + WIDTH)
        msq = square + column_ref[:, lanes]
        scaled = (coulomb / NG**3) / jnp.maximum(msq, 1.0)
        value = jnp.dot(low_ref[...], spec_ref[:, lanes], preferred_element_type=jnp.float32)
        value = value * jnp.where(msq > 0.0, scaled, 0.0)
        high = value.astype(jnp.bfloat16)
        low = (value - high.astype(jnp.float32)).astype(jnp.bfloat16)
        operand = jnp.concatenate([high, low, high], axis=0)
        result = jnp.dot(wide_ref[:rows], operand, preferred_element_type=jnp.float32)
        spec_ref[:rows, lanes] = result.astype(jnp.bfloat16)


def inverse(spec_ref, first_row, plane_ref, scratch, use):
    for first in range(0, BLOCKS, CHUNK):
        operand = jnp.concatenate(
            [
                spec_ref[first_row : first_row + ROWS, lane_block(first + b)]
                for b in range(CHUNK)
            ],
            axis=0,
        )
        both = jnp.dot(operand, plane_ref[:LANES], preferred_element_type=jnp.float32)
        scratch[first * ROWS : (first + CHUNK) * ROWS, :] = both[:, :LANES] + both[:, LANES:]
    for tile in range(ROWS // 8):
        fields = [
            scratch[b * ROWS + 8 * tile : b * ROWS + 8 * tile + 8, :] for b in range(BLOCKS)
        ]
        for b, item in enumerate(hartley(twist(fields))):
            use(slice(8 * tile, 8 * tile + 8), lane_block(b), item)


def near_kernel(same_ref, psi_ref, plane_ref, same_out, spec_out, scratch):
    same_out[...] = decoded(same_ref[...])
    forward(psi_ref.at[0], same_out, plane_ref, spec_out, 0, scratch)


def pair_kernel(cross_ref, beside_code, spec_in, plane_ref, low_ref, wide_ref, column_ref,
                field_out, spec_out, beside_out, cross_out, other, spec, scratch, sums):
    spec[:ROWS] = spec_in[...]
    other[...] = decoded(cross_ref[:, :PLANE])
    field_out[...] = decoded(beside_code[:, :PLANE])
    forward(field_out, other, plane_ref, spec, ROWS, scratch)
    screen(spec, low_ref, wide_ref, column_ref, NG)
    spec_out[...] = spec[:ROWS]

    def use(rows, lanes, item):
        sums[0, rows, lanes] = other[rows, lanes] * item
        sums[1, rows, lanes] = field_out[rows, lanes] * item

    inverse(spec, ROWS, plane_ref, scratch, use)
    beside_out[...] = sums[0].astype(jnp.bfloat16)
    cross_out[:, :PLANE] = sums[1].astype(jnp.bfloat16)
    cross_out[:, PLANE:] = jnp.zeros((ROWS, LANES), jnp.bfloat16)


def same_kernel(spec_ref, plane_ref, psi_ref, other_ref, part_out, same_out, scratch, total):
    def use(rows, lanes, item):
        part_out[rows, lanes] = other_ref[rows, lanes] * item
        total[rows, lanes] = psi_ref[0, rows, lanes] * item

    inverse(spec_ref, 0, plane_ref, scratch, use)
    same_out[...] = total[...].astype(jnp.bfloat16)


def self_kernel(psi_ref, mine_ref, beside_code, field_ref, plane_ref, low_ref, wide_ref,
                column_ref, part_ref, total_out, spec, scratch):
    forward(psi_ref.at[0], psi_ref.at[0], plane_ref, spec, 0, scratch)
    forward(field_ref, field_ref, plane_ref, spec, ROWS, scratch)
    first = lax.broadcasted_iota(jnp.int32, (ROWS, LANES), 1) == 0
    for rows, ref in ((slice(0, ROWS), mine_ref), (slice(ROWS, NG), beside_code)):
        spec[rows, :LANES] = jnp.where(first, ref[:, PLANE:], spec[rows, :LANES])
    screen(spec, low_ref, wide_ref, column_ref, ROWS)

    def use(rows, lanes, item):
        total_out[rows, lanes] = part_ref[rows, lanes] + psi_ref[0, rows, lanes] * item

    inverse(spec, 0, plane_ref, scratch, use)


vmem = pl.BlockSpec(memory_space=pltpu.VMEM)
limit = pltpu.CompilerParams(vmem_limit_bytes=14 * 1024 * 1024)


def shape(dims, dtype):
    return jax.ShapeDtypeStruct(dims, dtype)


def call(kernel, outs, *args, scratch=()):
    return pl.pallas_call(
        kernel, out_shape=outs, in_specs=[vmem] * len(args),
        out_specs=jax.tree.map(lambda _: vmem, outs),
        scratch_shapes=scratch, compiler_params=limit,
    )(*args)


def on_device(orbitals):
    bands = lax.axis_size("band")
    axes = ("band", "grid")

    def route(flip):
        pairs = []
        for band in range(bands):
            for g in range(2):
                other = (band - (1 if g == NEAR else REACH)) % bands
                pairs.append((2 * other + (1 - g if flip else g), 2 * band + g))
        return pairs

    def home(flip):
        return [(b, a) for a, b in route(flip)]

    swap = [(0, 1), (1, 0)]
    plane = jnp.asarray(plane_matrix())
    stacked = jnp.concatenate([plane, plane], axis=0)
    x_low, x_wide = (jnp.asarray(m) for m in x_matrices())
    column = jnp.asarray(column_squares())
    tables = (stacked, x_low, x_wide, column)

    sent = shape((ROWS, PLANE), jnp.bfloat16)
    field = shape((ROWS, PLANE), jnp.float32)
    spec = pltpu.VMEM((NG, PLANE), jnp.bfloat16)
    work = pltpu.VMEM((BLOCKS * ROWS, LANES), jnp.float32)
    marks = shape((ROWS, PLANE + LANES), jnp.bfloat16)

    code, wide = call(
        encode_kernel, (sent, shape((ROWS, PLANE + 2 * LANES), jnp.bfloat16)), orbitals
    )
    marked = call(
        mark_kernel, marks, orbitals, code,
        scratch=[pltpu.VMEM((BLOCKS * ROWS, LANES), jnp.float32)],
    )
    same = lax.ppermute(code, axes, route(False))
    cross = lax.ppermute(wide, axes, route(True))
    beside = lax.ppermute(marked, "grid", swap)
    other, top = call(near_kernel, (field, sent), same, orbitals, stacked, scratch=[work])
    partner, top, beside_share, cross = call(
        pair_kernel, (field, sent, sent, marks), cross, beside, top, *tables,
        scratch=[
            pltpu.VMEM((ROWS, PLANE), jnp.float32), spec, work,
            pltpu.VMEM((2, ROWS, PLANE), jnp.float32),
        ],
    )
    part, same = call(
        same_kernel, (field, sent), top, stacked, orbitals, other,
        scratch=[work, pltpu.VMEM((ROWS, PLANE), jnp.float32)],
    )
    total = call(
        self_kernel, field, orbitals, marked, beside, partner, *tables, part,
        scratch=[spec, work],
    )
    for share in (
        lax.ppermute(cross, axes, home(True))[:, :PLANE],
        lax.ppermute(beside_share, "grid", swap),
        lax.ppermute(same, axes, home(False)),
    ):
        total = total + share.astype(jnp.float32)
    return -total[None]


def solution(mesh):
    in_specs = (P("band", "grid", None),)
    out_specs = P("band", "grid", None)
    return jax.shard_map(
        on_device, mesh=mesh, in_specs=in_specs, out_specs=out_specs, check_vma=False
    )
```

```python
import math

import jax
import jax.numpy as jnp
import numpy as np
from jax import lax
from jax.experimental import pallas as pl
from jax.experimental.pallas import tpu as pltpu
from jax.sharding import PartitionSpec as P

NG = 64
REACH = 2
NEAR = 0
ROWS = NG // 2
PLANE = NG * NG
LANES = 2 * NG
BLOCKS = PLANE // LANES
CODE = 64.0
CHUNK = 16
WIDTH = 2048
coulomb = 46.9 * 46.9 / math.pi


def cas_table():
    count = np.arange(NG)
    angle = 2.0 * math.pi / NG * (count[:, None] * count[None, :] % NG)
    return np.cos(angle) + np.sin(angle)


def split(table):
    high = table.astype(jnp.bfloat16)
    low = (table - high.astype(np.float64)).astype(jnp.bfloat16)
    return high, low


def plane_matrix():
    cas = cas_table()
    high, low = split(np.block([[cas, cas], [cas, -cas]]))
    return np.concatenate([high, low], axis=1)


def x_matrices():
    cas = cas_table()
    high, low = split(cas)
    return high, np.concatenate([high, high, low], axis=1)


def column_squares():
    count = np.arange(NG)
    folded = np.where(count < NG // 2, count, count - NG)
    square = (folded * folded).astype(np.float32)
    block, upper, last = np.meshgrid(
        np.arange(BLOCKS), np.arange(2), np.arange(NG), indexing="ij"
    )
    return (square[block + BLOCKS * upper] + square[last]).reshape(1, PLANE)


def hartley(items):
    n = len(items)
    if n == 1:
        return items
    even, odd = hartley(items[0::2]), hartley(items[1::2])
    half = n // 2
    turned = list(odd)
    for k in range(1, (half + 1) // 2):
        c, s = math.cos(2.0 * math.pi * k / n), math.sin(2.0 * math.pi * k / n)
        a, b = odd[k], odd[half - k]
        if 8 * k == n:
            turned[k], turned[half - k] = (a + b) * c, (a - b) * c
        else:
            turned[k], turned[half - k] = a * c + b * s, a * s - b * c
    return [e + t for e, t in zip(even, turned)] + [e - t for e, t in zip(even, turned)]


def twist(items):
    n = len(items)
    low_lanes = lax.broadcasted_iota(jnp.int32, items[0].shape, 1) < NG
    out = [None] * n
    out[0] = items[0]
    for k in range(1, n // 2):
        c, s = math.cos(math.pi * k / n), math.sin(math.pi * k / n)
        a, b = items[k], items[n - k]
        out[k] = jnp.where(low_lanes, a, a * c + b * s)
        out[n - k] = jnp.where(low_lanes, b, a * s - b * c)
    out[n // 2] = items[n // 2]
    return out


def decoded(code):
    return jnp.log2(code.astype(jnp.float32)) * (1.0 / CODE)


def lane_block(b):
    return slice(b * LANES, (b + 1) * LANES)


def encode_kernel(psi_ref, code_ref, wide_ref):
    code = jnp.exp2(psi_ref[0] * CODE).astype(jnp.bfloat16)
    code_ref[...] = code
    wide_ref[:, :PLANE] = code
    wide_ref[:, PLANE:] = jnp.zeros((ROWS, 2 * LANES), jnp.bfloat16)


def mark_kernel(psi_ref, code_ref, marked_ref, turned):
    group = LANES // ROWS
    for t in range(BLOCKS // group):
        squares = [psi_ref[0, :, lane_block(t * group + k)] ** 2 for k in range(group)]
        turned[t * LANES : (t + 1) * LANES, :] = jnp.concatenate(squares, axis=0).T
    chains = 2 * BLOCKS // group
    along_z = turned[pl.ds(0, chains, stride=NG), :]
    for z in range(1, NG):
        along_z = along_z + turned[pl.ds(z, chains, stride=NG), :]
    shifted = [along_z] + [
        pltpu.roll(along_z, LANES - k * ROWS, axis=1) for k in range(1, group)
    ]
    total = None
    for t in range(BLOCKS // group):
        for k in range(group):
            for e in range(2):
                row = shifted[k][2 * t + e : 2 * t + e + 1]
                total = row if total is None else total + row
    marked_ref[:, :PLANE] = code_ref[...]
    column = jnp.broadcast_to(total, (LANES, LANES)).T[:ROWS]
    marked_ref[:, PLANE:] = column.astype(jnp.bfloat16)


def forward(mine, other, plane_ref, spec_ref, first_row, scratch):
    for tile in range(ROWS // 8):
        rows = slice(8 * tile, 8 * tile + 8)
        fields = [mine[rows, lane_block(b)] * other[rows, lane_block(b)] for b in range(BLOCKS)]
        for b, item in enumerate(twist(hartley(fields))):
            scratch[b * ROWS + 8 * tile : b * ROWS + 8 * tile + 8, :] = item
    for first in range(0, BLOCKS, CHUNK):
        value = scratch[first * ROWS : (first + CHUNK) * ROWS, :]
        high = value.astype(jnp.bfloat16)
        low = (value - high.astype(jnp.float32)).astype(jnp.bfloat16)
        operand = jnp.concatenate([high, low], axis=1)
        both = jnp.dot(operand, plane_ref[...], preferred_element_type=jnp.float32)
        spec = (both[:, :LANES] + both[:, LANES:]).astype(jnp.bfloat16)
        for b in range(CHUNK):
            spec_ref[first_row : first_row + ROWS, lane_block(first + b)] = (
                spec[b * ROWS : (b + 1) * ROWS]
            )


def screen(spec_ref, low_ref, wide_ref, column_ref, rows):
    count = lax.broadcasted_iota(jnp.int32, (NG, WIDTH), 0)
    folded = jnp.where(count < NG // 2, count, count - NG)
    square = (folded * folded).astype(jnp.float32)
    for first in range(0, PLANE, WIDTH):
        lanes = slice(first, first + WIDTH)
        msq = square + column_ref[:, lanes]
        scaled = (coulomb / NG**3) / jnp.maximum(msq, 1.0)
        value = jnp.dot(low_ref[...], spec_ref[:, lanes], preferred_element_type=jnp.float32)
        value = value * jnp.where(msq > 0.0, scaled, 0.0)
        high = value.astype(jnp.bfloat16)
        low = (value - high.astype(jnp.float32)).astype(jnp.bfloat16)
        operand = jnp.concatenate([high, low, high], axis=0)
        result = jnp.dot(wide_ref[:rows], operand, preferred_element_type=jnp.float32)
        spec_ref[:rows, lanes] = result.astype(jnp.bfloat16)


def inverse(spec_ref, first_row, plane_ref, scratch, use):
    for first in range(0, BLOCKS, CHUNK):
        operand = jnp.concatenate(
            [
                spec_ref[first_row : first_row + ROWS, lane_block(first + b)]
                for b in range(CHUNK)
            ],
            axis=0,
        )
        both = jnp.dot(operand, plane_ref[:LANES], preferred_element_type=jnp.float32)
        scratch[first * ROWS : (first + CHUNK) * ROWS, :] = both[:, :LANES] + both[:, LANES:]
    for tile in range(ROWS // 8):
        fields = [
            scratch[b * ROWS + 8 * tile : b * ROWS + 8 * tile + 8, :] for b in range(BLOCKS)
        ]
        for b, item in enumerate(hartley(twist(fields))):
            use(slice(8 * tile, 8 * tile + 8), lane_block(b), item)


def near_kernel(same_ref, psi_ref, plane_ref, same_out, spec_out, scratch):
    same_out[...] = decoded(same_ref[...])
    forward(psi_ref.at[0], same_out, plane_ref, spec_out, 0, scratch)


def pair_kernel(cross_ref, beside_code, spec_in, plane_ref, low_ref, wide_ref, column_ref,
                field_out, spec_out, beside_out, cross_out, other, spec, scratch, sums):
    spec[:ROWS] = spec_in[...]
    other[...] = decoded(cross_ref[:, :PLANE])
    field_out[...] = decoded(beside_code[:, :PLANE])
    forward(field_out, other, plane_ref, spec, ROWS, scratch)
    screen(spec, low_ref, wide_ref, column_ref, NG)
    spec_out[...] = spec[:ROWS]

    def use(rows, lanes, item):
        sums[0, rows, lanes] = other[rows, lanes] * item
        sums[1, rows, lanes] = field_out[rows, lanes] * item

    inverse(spec, ROWS, plane_ref, scratch, use)
    beside_out[...] = sums[0].astype(jnp.bfloat16)
    cross_out[:, :PLANE] = sums[1].astype(jnp.bfloat16)
    cross_out[:, PLANE:] = jnp.zeros((ROWS, LANES), jnp.bfloat16)


def same_kernel(spec_ref, plane_ref, psi_ref, other_ref, part_out, same_out, scratch, total):
    def use(rows, lanes, item):
        part_out[rows, lanes] = other_ref[rows, lanes] * item
        total[rows, lanes] = psi_ref[0, rows, lanes] * item

    inverse(spec_ref, 0, plane_ref, scratch, use)
    same_out[...] = total[...].astype(jnp.bfloat16)


def self_kernel(psi_ref, mine_ref, beside_code, field_ref, plane_ref, low_ref, wide_ref,
                column_ref, part_ref, total_out, spec, scratch):
    forward(psi_ref.at[0], psi_ref.at[0], plane_ref, spec, 0, scratch)
    forward(field_ref, field_ref, plane_ref, spec, ROWS, scratch)
    first = lax.broadcasted_iota(jnp.int32, (ROWS, LANES), 1) == 0
    for rows, ref in ((slice(0, ROWS), mine_ref), (slice(ROWS, NG), beside_code)):
        spec[rows, :LANES] = jnp.where(first, ref[:, PLANE:], spec[rows, :LANES])
    screen(spec, low_ref, wide_ref, column_ref, ROWS)

    def use(rows, lanes, item):
        total_out[rows, lanes] = part_ref[rows, lanes] + psi_ref[0, rows, lanes] * item

    inverse(spec, 0, plane_ref, scratch, use)


vmem = pl.BlockSpec(memory_space=pltpu.VMEM)
limit = pltpu.CompilerParams(vmem_limit_bytes=14 * 1024 * 1024)


def shape(dims, dtype):
    return jax.ShapeDtypeStruct(dims, dtype)


def call(kernel, outs, *args, scratch=()):
    return pl.pallas_call(
        kernel, out_shape=outs, in_specs=[vmem] * len(args),
        out_specs=jax.tree.map(lambda _: vmem, outs),
        scratch_shapes=scratch, compiler_params=limit,
    )(*args)


def on_device(orbitals):
    bands = lax.axis_size("band")
    axes = ("band", "grid")

    def route(flip):
        pairs = []
        for band in range(bands):
            for g in range(2):
                other = (band - (1 if g == NEAR else REACH)) % bands
                pairs.append((2 * other + (1 - g if flip else g), 2 * band + g))
        return pairs

    def home(flip):
        return [(b, a) for a, b in route(flip)]

    swap = [(0, 1), (1, 0)]
    plane = jnp.asarray(plane_matrix())
    stacked = jnp.concatenate([plane, plane], axis=0)
    x_low, x_wide = (jnp.asarray(m) for m in x_matrices())
    column = jnp.asarray(column_squares())
    tables = (stacked, x_low, x_wide, column)

    sent = shape((ROWS, PLANE), jnp.bfloat16)
    field = shape((ROWS, PLANE), jnp.float32)
    spec = pltpu.VMEM((NG, PLANE), jnp.bfloat16)
    work = pltpu.VMEM((BLOCKS * ROWS, LANES), jnp.float32)
    marks = shape((ROWS, PLANE + LANES), jnp.bfloat16)

    code, wide = call(
        encode_kernel, (sent, shape((ROWS, PLANE + 2 * LANES), jnp.bfloat16)), orbitals
    )
    marked = call(
        mark_kernel, marks, orbitals, code,
        scratch=[pltpu.VMEM((BLOCKS * ROWS, LANES), jnp.float32)],
    )
    same = lax.ppermute(code, axes, route(False))
    cross = lax.ppermute(wide, axes, route(True))
    beside = lax.ppermute(marked, "grid", swap)
    other, top = call(near_kernel, (field, sent), same, orbitals, stacked, scratch=[work])
    partner, top, beside_share, cross = call(
        pair_kernel, (field, sent, sent, marks), cross, beside, top, *tables,
        scratch=[
            pltpu.VMEM((ROWS, PLANE), jnp.float32), spec, work,
            pltpu.VMEM((2, ROWS, PLANE), jnp.float32),
        ],
    )
    part, same = call(
        same_kernel, (field, sent), top, stacked, orbitals, other,
        scratch=[work, pltpu.VMEM((ROWS, PLANE), jnp.float32)],
    )
    total = call(
        self_kernel, field, orbitals, marked, beside, partner, *tables, part,
        scratch=[spec, work],
    )
    for share in (
        lax.ppermute(cross, axes, home(True))[:, :PLANE],
        lax.ppermute(beside_share, "grid", swap),
        lax.ppermute(same, axes, home(False)),
    ):
        total = total + share.astype(jnp.float32)
    return -total[None]


def solution(mesh):
    in_specs = (P("band", "grid", None),)
    out_specs = P("band", "grid", None)
    return jax.shard_map(
        on_device, mesh=mesh, in_specs=in_specs, out_specs=out_specs, check_vma=False
    )
```

```python
import math

import jax
import jax.numpy as jnp
import numpy as np
from jax import lax
from jax.experimental import pallas as pl
from jax.experimental.pallas import tpu as pltpu
from jax.sharding import PartitionSpec as P

NG = 64
REACH = 2
NEAR = 0
ROWS = NG // 2
PLANE = NG * NG
LANES = 2 * NG
BLOCKS = PLANE // LANES
CODE = 64.0
CHUNK = 16
WIDTH = 2048
coulomb = 46.9 * 46.9 / math.pi


def cas_table():
    count = np.arange(NG)
    angle = 2.0 * math.pi / NG * (count[:, None] * count[None, :] % NG)
    return np.cos(angle) + np.sin(angle)


def split(table):
    high = table.astype(jnp.bfloat16)
    low = (table - high.astype(np.float64)).astype(jnp.bfloat16)
    return high, low


def plane_matrix():
    cas = cas_table()
    high, low = split(np.block([[cas, cas], [cas, -cas]]))
    return np.concatenate([high, low], axis=1)


def x_matrices():
    cas = cas_table()
    high, low = split(cas)
    return high, np.concatenate([high, high, low], axis=1)


def column_squares():
    count = np.arange(NG)
    folded = np.where(count < NG // 2, count, count - NG)
    square = (folded * folded).astype(np.float32)
    block, upper, last = np.meshgrid(
        np.arange(BLOCKS), np.arange(2), np.arange(NG), indexing="ij"
    )
    return (square[block + BLOCKS * upper] + square[last]).reshape(1, PLANE)


def hartley(items):
    n = len(items)
    if n == 1:
        return items
    even, odd = hartley(items[0::2]), hartley(items[1::2])
    half = n // 2
    turned = list(odd)
    for k in range(1, (half + 1) // 2):
        c, s = math.cos(2.0 * math.pi * k / n), math.sin(2.0 * math.pi * k / n)
        a, b = odd[k], odd[half - k]
        if 8 * k == n:
            turned[k], turned[half - k] = (a + b) * c, (a - b) * c
        else:
            turned[k], turned[half - k] = a * c + b * s, a * s - b * c
    return [e + t for e, t in zip(even, turned)] + [e - t for e, t in zip(even, turned)]


def twist(items):
    n = len(items)
    low_lanes = lax.broadcasted_iota(jnp.int32, items[0].shape, 1) < NG
    out = [None] * n
    out[0] = items[0]
    for k in range(1, n // 2):
        c, s = math.cos(math.pi * k / n), math.sin(math.pi * k / n)
        a, b = items[k], items[n - k]
        out[k] = jnp.where(low_lanes, a, a * c + b * s)
        out[n - k] = jnp.where(low_lanes, b, a * s - b * c)
    out[n // 2] = items[n // 2]
    return out


def decoded(code):
    return jnp.log2(code.astype(jnp.float32)) * (1.0 / CODE)


def lane_block(b):
    return slice(b * LANES, (b + 1) * LANES)


def encode_kernel(psi_ref, code_ref, wide_ref):
    code = jnp.exp2(psi_ref[0] * CODE).astype(jnp.bfloat16)
    code_ref[...] = code
    wide_ref[:, :PLANE] = code
    wide_ref[:, PLANE:] = jnp.zeros((ROWS, 2 * LANES), jnp.bfloat16)


def mark_kernel(psi_ref, code_ref, marked_ref, turned):
    group = LANES // ROWS
    for t in range(BLOCKS // group):
        squares = [psi_ref[0, :, lane_block(t * group + k)] ** 2 for k in range(group)]
        turned[t * LANES : (t + 1) * LANES, :] = jnp.concatenate(squares, axis=0).T
    chains = 2 * BLOCKS // group
    along_z = turned[pl.ds(0, chains, stride=NG), :]
    for z in range(1, NG):
        along_z = along_z + turned[pl.ds(z, chains, stride=NG), :]
    shifted = [along_z] + [
        pltpu.roll(along_z, LANES - k * ROWS, axis=1) for k in range(1, group)
    ]
    total = None
    for t in range(BLOCKS // group):
        for k in range(group):
            for e in range(2):
                row = shifted[k][2 * t + e : 2 * t + e + 1]
                total = row if total is None else total + row
    marked_ref[:, :PLANE] = code_ref[...]
    column = jnp.broadcast_to(total, (LANES, LANES)).T[:ROWS]
    marked_ref[:, PLANE:] = column.astype(jnp.bfloat16)


def forward(mine, other, plane_ref, spec_ref, first_row, scratch):
    for tile in range(ROWS // 8):
        rows = slice(8 * tile, 8 * tile + 8)
        fields = [mine[rows, lane_block(b)] * other[rows, lane_block(b)] for b in range(BLOCKS)]
        for b, item in enumerate(twist(hartley(fields))):
            scratch[b * ROWS + 8 * tile : b * ROWS + 8 * tile + 8, :] = item
    for first in range(0, BLOCKS, CHUNK):
        value = scratch[first * ROWS : (first + CHUNK) * ROWS, :]
        high = value.astype(jnp.bfloat16)
        low = (value - high.astype(jnp.float32)).astype(jnp.bfloat16)
        operand = jnp.concatenate([high, low], axis=1)
        both = jnp.dot(operand, plane_ref[...], preferred_element_type=jnp.float32)
        spec = (both[:, :LANES] + both[:, LANES:]).astype(jnp.bfloat16)
        for b in range(CHUNK):
            spec_ref[first_row : first_row + ROWS, lane_block(first + b)] = (
                spec[b * ROWS : (b + 1) * ROWS]
            )


def screen(spec_ref, low_ref, wide_ref, column_ref, rows):
    count = lax.broadcasted_iota(jnp.int32, (NG, WIDTH), 0)
    folded = jnp.where(count < NG // 2, count, count - NG)
    square = (folded * folded).astype(jnp.float32)
    for first in range(0, PLANE, WIDTH):
        lanes = slice(first, first + WIDTH)
        msq = square + column_ref[:, lanes]
        scaled = (coulomb / NG**3) / jnp.maximum(msq, 1.0)
        value = jnp.dot(low_ref[...], spec_ref[:, lanes], preferred_element_type=jnp.float32)
        value = value * jnp.where(msq > 0.0, scaled, 0.0)
        high = value.astype(jnp.bfloat16)
        low = (value - high.astype(jnp.float32)).astype(jnp.bfloat16)
        operand = jnp.concatenate([high, low, high], axis=0)
        result = jnp.dot(wide_ref[:rows], operand, preferred_element_type=jnp.float32)
        spec_ref[:rows, lanes] = result.astype(jnp.bfloat16)


def inverse(spec_ref, first_row, plane_ref, scratch, use):
    for first in range(0, BLOCKS, CHUNK):
        operand = jnp.concatenate(
            [
                spec_ref[first_row : first_row + ROWS, lane_block(first + b)]
                for b in range(CHUNK)
            ],
            axis=0,
        )
        both = jnp.dot(operand, plane_ref[:LANES], preferred_element_type=jnp.float32)
        scratch[first * ROWS : (first + CHUNK) * ROWS, :] = both[:, :LANES] + both[:, LANES:]
    for tile in range(ROWS // 8):
        fields = [
            scratch[b * ROWS + 8 * tile : b * ROWS + 8 * tile + 8, :] for b in range(BLOCKS)
        ]
        for b, item in enumerate(hartley(twist(fields))):
            use(slice(8 * tile, 8 * tile + 8), lane_block(b), item)


def near_kernel(same_ref, cross_ref, psi_ref, plane_ref, same_out, cross_out, spec_out, scratch):
    same_out[...] = decoded(same_ref[...])
    cross_out[...] = decoded(cross_ref[:, :PLANE])
    forward(psi_ref.at[0], same_out, plane_ref, spec_out, 0, scratch)


def pair_kernel(other, beside_code, spec_in, plane_ref, low_ref, wide_ref, column_ref,
                field_out, spec_out, beside_out, cross_out, spec, scratch, sums):
    spec[:ROWS] = spec_in[...]
    field_out[...] = decoded(beside_code[:, :PLANE])
    forward(field_out, other, plane_ref, spec, ROWS, scratch)
    screen(spec, low_ref, wide_ref, column_ref, NG)
    spec_out[...] = spec[:ROWS]

    def use(rows, lanes, item):
        sums[0, rows, lanes] = other[rows, lanes] * item
        sums[1, rows, lanes] = field_out[rows, lanes] * item

    inverse(spec, ROWS, plane_ref, scratch, use)
    beside_out[...] = sums[0].astype(jnp.bfloat16)
    cross_out[:, :PLANE] = sums[1].astype(jnp.bfloat16)
    cross_out[:, PLANE:] = jnp.zeros((ROWS, LANES), jnp.bfloat16)


def same_kernel(spec_ref, plane_ref, psi_ref, other_ref, part_out, same_out, scratch, total):
    def use(rows, lanes, item):
        part_out[rows, lanes] = other_ref[rows, lanes] * item
        total[rows, lanes] = psi_ref[0, rows, lanes] * item

    inverse(spec_ref, 0, plane_ref, scratch, use)
    same_out[...] = total[...].astype(jnp.bfloat16)


def self_kernel(psi_ref, mine_ref, beside_code, field_ref, plane_ref, low_ref, wide_ref,
                column_ref, part_ref, total_out, spec, scratch):
    forward(psi_ref.at[0], psi_ref.at[0], plane_ref, spec, 0, scratch)
    forward(field_ref, field_ref, plane_ref, spec, ROWS, scratch)
    first = lax.broadcasted_iota(jnp.int32, (ROWS, LANES), 1) == 0
    for rows, ref in ((slice(0, ROWS), mine_ref), (slice(ROWS, NG), beside_code)):
        spec[rows, :LANES] = jnp.where(first, ref[:, PLANE:], spec[rows, :LANES])
    screen(spec, low_ref, wide_ref, column_ref, ROWS)

    def use(rows, lanes, item):
        total_out[rows, lanes] = part_ref[rows, lanes] + psi_ref[0, rows, lanes] * item

    inverse(spec, 0, plane_ref, scratch, use)


vmem = pl.BlockSpec(memory_space=pltpu.VMEM)
limit = pltpu.CompilerParams(vmem_limit_bytes=14 * 1024 * 1024)


def shape(dims, dtype):
    return jax.ShapeDtypeStruct(dims, dtype)


def call(kernel, outs, *args, scratch=()):
    return pl.pallas_call(
        kernel, out_shape=outs, in_specs=[vmem] * len(args),
        out_specs=jax.tree.map(lambda _: vmem, outs),
        scratch_shapes=scratch, compiler_params=limit,
    )(*args)


def on_device(orbitals):
    bands = lax.axis_size("band")
    axes = ("band", "grid")

    def route(flip):
        pairs = []
        for band in range(bands):
            for g in range(2):
                other = (band - (1 if g == NEAR else REACH)) % bands
                pairs.append((2 * other + (1 - g if flip else g), 2 * band + g))
        return pairs

    def home(flip):
        return [(b, a) for a, b in route(flip)]

    swap = [(0, 1), (1, 0)]
    plane = jnp.asarray(plane_matrix())
    stacked = jnp.concatenate([plane, plane], axis=0)
    x_low, x_wide = (jnp.asarray(m) for m in x_matrices())
    column = jnp.asarray(column_squares())
    tables = (stacked, x_low, x_wide, column)

    sent = shape((ROWS, PLANE), jnp.bfloat16)
    field = shape((ROWS, PLANE), jnp.float32)
    spec = pltpu.VMEM((NG, PLANE), jnp.bfloat16)
    work = pltpu.VMEM((BLOCKS * ROWS, LANES), jnp.float32)
    marks = shape((ROWS, PLANE + LANES), jnp.bfloat16)

    code, wide = call(
        encode_kernel, (sent, shape((ROWS, PLANE + 2 * LANES), jnp.bfloat16)), orbitals
    )
    marked = call(
        mark_kernel, marks, orbitals, code,
        scratch=[pltpu.VMEM((BLOCKS * ROWS, LANES), jnp.float32)],
    )
    same = lax.ppermute(code, axes, route(False))
    cross = lax.ppermute(wide, axes, route(True))
    beside = lax.ppermute(marked, "grid", swap)
    other, beyond, top = call(
        near_kernel, (field, field, sent), same, cross, orbitals, stacked, scratch=[work]
    )
    partner, top, beside_share, cross = call(
        pair_kernel, (field, sent, sent, marks), beyond, beside, top, *tables,
        scratch=[
            spec, work,
            pltpu.VMEM((2, ROWS, PLANE), jnp.float32),
        ],
    )
    part, same = call(
        same_kernel, (field, sent), top, stacked, orbitals, other,
        scratch=[work, pltpu.VMEM((ROWS, PLANE), jnp.float32)],
    )
    total = call(
        self_kernel, field, orbitals, marked, beside, partner, *tables, part,
        scratch=[spec, work],
    )
    for share in (
        lax.ppermute(cross, axes, home(True))[:, :PLANE],
        lax.ppermute(beside_share, "grid", swap),
        lax.ppermute(same, axes, home(False)),
    ):
        total = total + share.astype(jnp.float32)
    return -total[None]


def solution(mesh):
    in_specs = (P("band", "grid", None),)
    out_specs = P("band", "grid", None)
    return jax.shard_map(
        on_device, mesh=mesh, in_specs=in_specs, out_specs=out_specs, check_vma=False
    )
```

```python
import math

import jax
import jax.numpy as jnp
import numpy as np
from jax import lax
from jax.experimental import pallas as pl
from jax.experimental.pallas import tpu as pltpu
from jax.sharding import PartitionSpec as P

NG = 64
REACH = 2
NEAR = 0
ROWS = NG // 2
PLANE = NG * NG
LANES = 2 * NG
BLOCKS = PLANE // LANES
CODE = 64.0
CHUNK = 32
WIDTH = 4096
coulomb = 46.9 * 46.9 / math.pi


def cas_table():
    count = np.arange(NG)
    angle = 2.0 * math.pi / NG * (count[:, None] * count[None, :] % NG)
    return np.cos(angle) + np.sin(angle)


def split(table):
    high = table.astype(jnp.bfloat16)
    low = (table - high.astype(np.float64)).astype(jnp.bfloat16)
    return high, low


def plane_matrix():
    cas = cas_table()
    high, low = split(np.block([[cas, cas], [cas, -cas]]))
    return np.concatenate([high, low], axis=1)


def x_matrices():
    cas = cas_table()
    high, low = split(cas)
    return high, np.concatenate([high, high, low], axis=1)


def column_squares():
    count = np.arange(NG)
    folded = np.where(count < NG // 2, count, count - NG)
    square = (folded * folded).astype(np.float32)
    block, upper, last = np.meshgrid(
        np.arange(BLOCKS), np.arange(2), np.arange(NG), indexing="ij"
    )
    return (square[block + BLOCKS * upper] + square[last]).reshape(1, PLANE)


def hartley(items):
    n = len(items)
    if n == 1:
        return items
    even, odd = hartley(items[0::2]), hartley(items[1::2])
    half = n // 2
    turned = list(odd)
    for k in range(1, (half + 1) // 2):
        c, s = math.cos(2.0 * math.pi * k / n), math.sin(2.0 * math.pi * k / n)
        a, b = odd[k], odd[half - k]
        if 8 * k == n:
            turned[k], turned[half - k] = (a + b) * c, (a - b) * c
        else:
            turned[k], turned[half - k] = a * c + b * s, a * s - b * c
    return [e + t for e, t in zip(even, turned)] + [e - t for e, t in zip(even, turned)]


def twist(items):
    n = len(items)
    low_lanes = lax.broadcasted_iota(jnp.int32, items[0].shape, 1) < NG
    out = [None] * n
    out[0] = items[0]
    for k in range(1, n // 2):
        c, s = math.cos(math.pi * k / n), math.sin(math.pi * k / n)
        a, b = items[k], items[n - k]
        out[k] = jnp.where(low_lanes, a, a * c + b * s)
        out[n - k] = jnp.where(low_lanes, b, a * s - b * c)
    out[n // 2] = items[n // 2]
    return out


def decoded(code):
    return jnp.log2(code.astype(jnp.float32)) * (1.0 / CODE)


def lane_block(b):
    return slice(b * LANES, (b + 1) * LANES)


def encode_kernel(psi_ref, code_ref, wide_ref):
    code = jnp.exp2(psi_ref[0] * CODE).astype(jnp.bfloat16)
    code_ref[...] = code
    wide_ref[:, :PLANE] = code
    wide_ref[:, PLANE:] = jnp.zeros((ROWS, 2 * LANES), jnp.bfloat16)


def mark_kernel(psi_ref, code_ref, marked_ref, turned):
    group = LANES // ROWS
    for t in range(BLOCKS // group):
        squares = [psi_ref[0, :, lane_block(t * group + k)] ** 2 for k in range(group)]
        turned[t * LANES : (t + 1) * LANES, :] = jnp.concatenate(squares, axis=0).T
    chains = 2 * BLOCKS // group
    along_z = turned[pl.ds(0, chains, stride=NG), :]
    for z in range(1, NG):
        along_z = along_z + turned[pl.ds(z, chains, stride=NG), :]
    shifted = [along_z] + [
        pltpu.roll(along_z, LANES - k * ROWS, axis=1) for k in range(1, group)
    ]
    total = None
    for t in range(BLOCKS // group):
        for k in range(group):
            for e in range(2):
                row = shifted[k][2 * t + e : 2 * t + e + 1]
                total = row if total is None else total + row
    marked_ref[:, :PLANE] = code_ref[...]
    column = jnp.broadcast_to(total, (LANES, LANES)).T[:ROWS]
    marked_ref[:, PLANE:] = column.astype(jnp.bfloat16)


def forward(mine, other, plane_ref, spec_ref, first_row, scratch):
    for tile in range(ROWS // 8):
        rows = slice(8 * tile, 8 * tile + 8)
        fields = [mine[rows, lane_block(b)] * other[rows, lane_block(b)] for b in range(BLOCKS)]
        for b, item in enumerate(twist(hartley(fields))):
            scratch[b * ROWS + 8 * tile : b * ROWS + 8 * tile + 8, :] = item
    for first in range(0, BLOCKS, CHUNK):
        value = scratch[first * ROWS : (first + CHUNK) * ROWS, :]
        high = value.astype(jnp.bfloat16)
        low = (value - high.astype(jnp.float32)).astype(jnp.bfloat16)
        operand = jnp.concatenate([high, low], axis=1)
        both = jnp.dot(operand, plane_ref[...], preferred_element_type=jnp.float32)
        spec = (both[:, :LANES] + both[:, LANES:]).astype(jnp.bfloat16)
        for b in range(CHUNK):
            spec_ref[first_row : first_row + ROWS, lane_block(first + b)] = (
                spec[b * ROWS : (b + 1) * ROWS]
            )


def screen(spec_ref, low_ref, wide_ref, column_ref, rows):
    count = lax.broadcasted_iota(jnp.int32, (NG, WIDTH), 0)
    folded = jnp.where(count < NG // 2, count, count - NG)
    square = (folded * folded).astype(jnp.float32)
    for first in range(0, PLANE, WIDTH):
        lanes = slice(first, first + WIDTH)
        msq = square + column_ref[:, lanes]
        scaled = (coulomb / NG**3) / jnp.maximum(msq, 1.0)
        value = jnp.dot(low_ref[...], spec_ref[:, lanes], preferred_element_type=jnp.float32)
        value = value * jnp.where(msq > 0.0, scaled, 0.0)
        high = value.astype(jnp.bfloat16)
        low = (value - high.astype(jnp.float32)).astype(jnp.bfloat16)
        operand = jnp.concatenate([high, low, high], axis=0)
        result = jnp.dot(wide_ref[:rows], operand, preferred_element_type=jnp.float32)
        spec_ref[:rows, lanes] = result.astype(jnp.bfloat16)


def inverse(spec_ref, first_row, plane_ref, scratch, use):
    for first in range(0, BLOCKS, CHUNK):
        operand = jnp.concatenate(
            [
                spec_ref[first_row : first_row + ROWS, lane_block(first + b)]
                for b in range(CHUNK)
            ],
            axis=0,
        )
        both = jnp.dot(operand, plane_ref[:LANES], preferred_element_type=jnp.float32)
        scratch[first * ROWS : (first + CHUNK) * ROWS, :] = both[:, :LANES] + both[:, LANES:]
    for tile in range(ROWS // 8):
        fields = [
            scratch[b * ROWS + 8 * tile : b * ROWS + 8 * tile + 8, :] for b in range(BLOCKS)
        ]
        for b, item in enumerate(hartley(twist(fields))):
            use(slice(8 * tile, 8 * tile + 8), lane_block(b), item)


def near_kernel(same_ref, cross_ref, psi_ref, plane_ref, same_out, cross_out, spec_out, scratch):
    same_out[...] = decoded(same_ref[...])
    cross_out[...] = decoded(cross_ref[:, :PLANE])
    forward(psi_ref.at[0], same_out, plane_ref, spec_out, 0, scratch)


def pair_kernel(other, beside_code, spec_in, plane_ref, low_ref, wide_ref, column_ref,
                field_out, spec_out, beside_out, cross_out, spec, scratch, sums):
    spec[:ROWS] = spec_in[...]
    field_out[...] = decoded(beside_code[:, :PLANE])
    forward(field_out, other, plane_ref, spec, ROWS, scratch)
    screen(spec, low_ref, wide_ref, column_ref, NG)
    spec_out[...] = spec[:ROWS]

    def use(rows, lanes, item):
        sums[0, rows, lanes] = other[rows, lanes] * item
        sums[1, rows, lanes] = field_out[rows, lanes] * item

    inverse(spec, ROWS, plane_ref, scratch, use)
    beside_out[...] = sums[0].astype(jnp.bfloat16)
    cross_out[:, :PLANE] = sums[1].astype(jnp.bfloat16)
    cross_out[:, PLANE:] = jnp.zeros((ROWS, LANES), jnp.bfloat16)


def same_kernel(spec_ref, plane_ref, psi_ref, other_ref, part_out, same_out, scratch, total):
    def use(rows, lanes, item):
        part_out[rows, lanes] = other_ref[rows, lanes] * item
        total[rows, lanes] = psi_ref[0, rows, lanes] * item

    inverse(spec_ref, 0, plane_ref, scratch, use)
    same_out[...] = total[...].astype(jnp.bfloat16)


def self_kernel(psi_ref, mine_ref, beside_code, field_ref, plane_ref, low_ref, wide_ref,
                column_ref, part_ref, total_out, spec, scratch):
    forward(psi_ref.at[0], psi_ref.at[0], plane_ref, spec, 0, scratch)
    forward(field_ref, field_ref, plane_ref, spec, ROWS, scratch)
    first = lax.broadcasted_iota(jnp.int32, (ROWS, LANES), 1) == 0
    for rows, ref in ((slice(0, ROWS), mine_ref), (slice(ROWS, NG), beside_code)):
        spec[rows, :LANES] = jnp.where(first, ref[:, PLANE:], spec[rows, :LANES])
    screen(spec, low_ref, wide_ref, column_ref, ROWS)

    def use(rows, lanes, item):
        total_out[rows, lanes] = part_ref[rows, lanes] + psi_ref[0, rows, lanes] * item

    inverse(spec, 0, plane_ref, scratch, use)


vmem = pl.BlockSpec(memory_space=pltpu.VMEM)
limit = pltpu.CompilerParams(vmem_limit_bytes=14 * 1024 * 1024)


def shape(dims, dtype):
    return jax.ShapeDtypeStruct(dims, dtype)


def call(kernel, outs, *args, scratch=()):
    return pl.pallas_call(
        kernel, out_shape=outs, in_specs=[vmem] * len(args),
        out_specs=jax.tree.map(lambda _: vmem, outs),
        scratch_shapes=scratch, compiler_params=limit,
    )(*args)


def on_device(orbitals):
    bands = lax.axis_size("band")
    axes = ("band", "grid")

    def route(flip):
        pairs = []
        for band in range(bands):
            for g in range(2):
                other = (band - (1 if g == NEAR else REACH)) % bands
                pairs.append((2 * other + (1 - g if flip else g), 2 * band + g))
        return pairs

    def home(flip):
        return [(b, a) for a, b in route(flip)]

    swap = [(0, 1), (1, 0)]
    plane = jnp.asarray(plane_matrix())
    stacked = jnp.concatenate([plane, plane], axis=0)
    x_low, x_wide = (jnp.asarray(m) for m in x_matrices())
    column = jnp.asarray(column_squares())
    tables = (stacked, x_low, x_wide, column)

    sent = shape((ROWS, PLANE), jnp.bfloat16)
    field = shape((ROWS, PLANE), jnp.float32)
    spec = pltpu.VMEM((NG, PLANE), jnp.bfloat16)
    work = pltpu.VMEM((BLOCKS * ROWS, LANES), jnp.float32)
    marks = shape((ROWS, PLANE + LANES), jnp.bfloat16)

    code, wide = call(
        encode_kernel, (sent, shape((ROWS, PLANE + 2 * LANES), jnp.bfloat16)), orbitals
    )
    marked = call(
        mark_kernel, marks, orbitals, code,
        scratch=[pltpu.VMEM((BLOCKS * ROWS, LANES), jnp.float32)],
    )
    same = lax.ppermute(code, axes, route(False))
    cross = lax.ppermute(wide, axes, route(True))
    beside = lax.ppermute(marked, "grid", swap)
    other, beyond, top = call(
        near_kernel, (field, field, sent), same, cross, orbitals, stacked, scratch=[work]
    )
    partner, top, beside_share, cross = call(
        pair_kernel, (field, sent, sent, marks), beyond, beside, top, *tables,
        scratch=[
            spec, work,
            pltpu.VMEM((2, ROWS, PLANE), jnp.float32),
        ],
    )
    part, same = call(
        same_kernel, (field, sent), top, stacked, orbitals, other,
        scratch=[work, pltpu.VMEM((ROWS, PLANE), jnp.float32)],
    )
    total = call(
        self_kernel, field, orbitals, marked, beside, partner, *tables, part,
        scratch=[spec, work],
    )
    for share in (
        lax.ppermute(cross, axes, home(True))[:, :PLANE],
        lax.ppermute(beside_share, "grid", swap),
        lax.ppermute(same, axes, home(False)),
    ):
        total = total + share.astype(jnp.float32)
    return -total[None]


def solution(mesh):
    in_specs = (P("band", "grid", None),)
    out_specs = P("band", "grid", None)
    return jax.shard_map(
        on_device, mesh=mesh, in_specs=in_specs, out_specs=out_specs, check_vma=False
    )
```
